32 devices in a mesh: groups: 2 (over x), expert: 16 (over z, y, core).
Axes of the slice: x: 2, y: 2, z: 4, core: 2. Of those that a mesh axis runs over, the one named last changes fastest.
Arguments:
- tokens: bfloat16 [1024, 3584], P(('groups', 'expert')), parts along dimension 0, may hold values from -6 to 6
- routes: int32 [1024, 8], P(('groups', 'expert')), parts along dimension 0, may hold values from 0 to 31, all different within a row; in each aligned block of 32 rows (0 to 31, 32 to 63, ...) at most 9 rows name the same one
- gate_code: int32 [1024, 8], P(('groups', 'expert')), parts along dimension 0, may hold values from 0 to 15
- base_weight: bfloat16 [3584, 1024], replicated, may hold values from -0.09375 to 0.09375
- delta_in: bfloat16 [32, 3584, 128], P('expert'), may hold values from -0.09375 to 0.09375
- delta_out: bfloat16 [32, 128, 1024], P('expert'), may hold values from -0.5 to 0.5
Outputs:
- combined: bfloat16 [1024, 1024], P(('groups', 'expert')), parts along dimension 0
The draws below stay inside these ranges and needn't reach their ends.
There are 2 independent parts, one for each index of `groups`. The reference program is written for one: setup_inputs(seed, part) draws one part's arguments, and reference() takes and returns one part's arrays. A program takes and returns all parts, laid end to end along the dimension named above; an argument that names none is the same for every part. Nothing has to cross between parts.
Inputs may be any that keep to these rules, and one draw needn't show every extreme that they name: `routes`: each row names 8 different experts; the rows of one device name any expert at most 9 times, a bound that some block reaches.
All inputs are finite; a program needn't handle non-finite values.
Results may differ from the reference program's by a relative error of at most 0.0065.
Values may be sent and summed in bfloat16 or wider, within the bound.
No kernel may reach another device: no remote copies, remote signals or barrier semaphores. Data moves between devices by JAX's collectives and lax.ppermute only.
A program may use at most 64 MiB of HBM per device.

```python
import math
import jax
import jax.numpy as jnp
import numpy as np
from jax import lax

D = 3584
FF = 1024
RANK = 128
TOP = 8
TOK_DEV = 32
E = 32
TOKENS = 512
CAP = 9
N_EXPERT = 16


def with_ends(result, own_key, least, high):
    longest = result.shape.index(max(result.shape))
    spots = []
    for shift in (0, 1):
        where = [jax.random.randint(jax.random.fold_in(own_key, axis), (), 0, length) for axis, length in enumerate(result.shape)]
        where[longest] = (where[longest] + shift) % result.shape[longest]
        spots.append(tuple(where))
    return result.at[spots[0]].set(least).at[spots[1]].set(high)


def levels(own_key, dims, cuts, smallest, high):
    level = 1.0
    for position, blocks in cuts:
        steps = jax.random.uniform(jax.random.fold_in(jax.random.fold_in(own_key, 6), position), (blocks,), jnp.float32, smallest / len(cuts), high / len(cuts))
        level = level * jnp.repeat(jnp.exp(steps), dims[position] // blocks).reshape((-1,) + (1,) * (len(dims) - 1 - position))
    return level


def shared_out(own_key, own, number, rows, amount, top, limit, slope):
    sequence = jax.random.permutation(own_key, amount)
    crowded, usual = portions_of(amount, rows * top, limit, slope, True), portions_of(amount, rows * top, limit, slope, False)
    places = jnp.arange(amount)

    def named(tallies, offset_by):
        used = int((tallies > 0).sum())
        fixed = max(1, used // 4)
        moved = fixed + (places - fixed + offset_by * (used - fixed)) % max(1, amount - fixed)
        return jnp.zeros((amount,), jnp.int32).at[sequence[jnp.where(places < fixed, places, moved)]].set(jnp.asarray(tallies, jnp.int32))

    tallies = jnp.where(number % 4 == 0, named(crowded, number // 4), named(usual, number - number // 4 - 1))
    mixed = jax.random.permutation(jax.random.fold_in(own, 3), amount)
    giver, receiver = mixed[0:amount // 2 * 2:2], mixed[1:amount // 2 * 2:2]
    room = jnp.minimum(tallies[giver] - 1, limit - tallies[receiver]) // 2
    room = jnp.where((giver == sequence[0]) | (receiver == sequence[0]) | (tallies[receiver] == 0), 0, jnp.maximum(room, 0))
    moved = jax.random.randint(jax.random.fold_in(own, 4), (amount // 2,), 0, 1 << 20) % (room + 1)
    tallies = tallies.at[giver].add(-moved).at[receiver].add(moved)
    items = jnp.searchsorted(jnp.cumsum(tallies), jnp.arange(rows * top), side="right").astype(jnp.int32)
    grid = items.reshape(top, rows).T
    grid = grid[jax.random.permutation(jax.random.fold_in(own, 1), rows)]
    offset_by = jax.random.randint(jax.random.fold_in(own, 2), (rows, 1), 0, top)
    return jnp.take_along_axis(grid, (jnp.arange(top)[None, :] + offset_by) % top, axis=1)


def portions_of(number_of, total, reach, lean, full):
    portions = [(1 << 20) // math.isqrt(grade ** lean) + 1 for grade in range(1, number_of + 1)]
    largest = reach if full else min(reach, max(-(-total // number_of), total * portions[0] // sum(portions)))
    least = 1 if total - largest >= number_of - 1 else 0
    holding, rest = [largest] + [least] * (number_of - 1), total - largest - least * (number_of - 1)
    while rest > 0:
        candidates = [i for i in range(1, number_of) if holding[i] < largest] or [i for i in range(1, number_of) if holding[i] < reach]
        pool, budget = sum([portions[i] for i in candidates]), rest
        for i in candidates:
            addition = min(reach - holding[i], max(1, budget * portions[i] // pool), rest)
            holding[i] = holding[i] + addition
            rest = rest - addition
    return np.array(holding)


def gaussian(own_key, extent, deviation, bound, cuts=(), held_as=jnp.bfloat16):
    result = jax.random.normal(own_key, extent, jnp.float32) * deviation
    if len(cuts) > 0:
        result = levels(own_key, extent, cuts, -0.22, 0.18) * result
    return jnp.clip(result, min=-bound, max=bound).astype(held_as)


def setup_inputs(seed: int = 0, part: int = 0) -> dict:
    key_of = jax.random.split(jax.random.key(seed), 7)
    own_keys = jax.random.split(jax.random.fold_in(key_of[6], part), 7)
    tokens = gaussian(own_keys[0], (TOKENS, D), 1.0, 6.0, ((0, 16),))
    routes_keys = jax.random.split(jax.random.fold_in(own_keys[1], 1), TOKENS // TOK_DEV)
    routes_turns = jax.random.permutation(jax.random.fold_in(own_keys[1], 3), TOKENS // TOK_DEV)
    routes = jax.vmap(lambda own, number: shared_out(jax.random.fold_in(own_keys[1], 2), own, number, TOK_DEV, E, TOP, CAP, 2))(routes_keys, routes_turns).reshape((TOKENS, TOP))
    gate_code = with_ends(jax.random.randint(own_keys[2], (TOKENS, TOP), 0, 16), jax.random.fold_in(own_keys[2], 1), 0, 15).astype(jnp.int32)
    base_weight = gaussian(key_of[3], (D, FF), D ** -0.5, 0.09375)
    delta_in = gaussian(key_of[4], (E, D, RANK), D ** -0.5, 0.09375, ((0, 16),))
    delta_out = gaussian(key_of[5], (E, RANK, FF), RANK ** -0.5, 0.5, ((0, 16),))
    return dict(tokens=tokens, routes=routes, gate_code=gate_code, base_weight=base_weight, delta_in=delta_in, delta_out=delta_out)


def reference(tokens, routes, gate_code, base_weight, delta_in, delta_out):
    experts = delta_in.shape[0]
    top_count = routes.shape[1]
    flat_routes = routes.reshape(-1)
    pair_count = flat_routes.shape[0]
    order = jnp.argsort(flat_routes, stable=True).astype(jnp.int32)
    counts = jnp.zeros((experts,), jnp.int32).at[flat_routes].add(1)
    starts = (jnp.cumsum(counts) - counts).astype(jnp.int32)
    most_rows = N_EXPERT * CAP
    padded = jnp.concatenate([order, jnp.zeros((most_rows,), jnp.int32)])

    def one_expert(carry, expert_id):
        where_pairs = lax.dynamic_slice_in_dim(padded, starts[expert_id], most_rows)
        rows = tokens[where_pairs // top_count]
        latent = jnp.dot(rows, delta_in[expert_id], preferred_element_type=jnp.float32).astype(jnp.bfloat16)
        change = jnp.dot(latent, delta_out[expert_id], preferred_element_type=jnp.float32).astype(jnp.bfloat16)
        change = change.astype(carry.dtype)
        valid = (jnp.arange(most_rows) < counts[expert_id])[:, None]
        return carry.at[where_pairs].add(jnp.where(valid, change, jnp.zeros_like(change))), None

    initial = jnp.zeros((pair_count, base_weight.shape[1]), jnp.float32)
    deltas, _ = lax.scan(one_expert, initial, jnp.arange(experts, dtype=jnp.int32))
    shared = jnp.dot(tokens, base_weight, preferred_element_type=jnp.float32)
    summed = shared[:, None, :] + deltas.reshape(tokens.shape[0], top_count, -1)
    hidden = jax.nn.silu(summed).astype(jnp.bfloat16)
    gate = (gate_code.astype(jnp.float32) + 1.0) / 16.0
    return jnp.sum(gate[:, :, None] * hidden.astype(jnp.float32), axis=1).astype(jnp.bfloat16)
```

```python
import functools
import jax
import jax.numpy as jnp
from jax import lax
from jax.experimental import pallas as pl
from jax.experimental.pallas import tpu as pltpu
from jax.sharding import PartitionSpec as P

gate_levels = 16.0
lanes = 128
vmem = pl.BlockSpec(memory_space=pltpu.VMEM)


def pack_body(tokens_ref, routes_ref, codes_ref, out_ref):
    features = tokens_ref.shape[1]
    rows, top_count = routes_ref.shape
    width = out_ref.shape[1] - features
    out_ref[:, :features] = tokens_ref[...]
    lane = lax.broadcasted_iota(jnp.int32, (rows, width), 1)
    gates = jnp.zeros((rows, width), jnp.float32)
    for k in range(top_count):
        weight = (codes_ref[:, k : k + 1].astype(jnp.float32) + 1.0) / gate_levels
        gates = gates + jnp.where(routes_ref[:, k : k + 1] == lane, weight, 0.0)
    out_ref[:, features:] = gates.astype(out_ref.dtype)


def expert_body(features, blocks, *refs):
    first_ref, x_refs = refs[0], refs[1 : 1 + blocks]
    base_ref, down_ref, up_own_ref, up_peer_ref = refs[1 + blocks : 5 + blocks]
    out_refs = refs[5 + blocks :]
    rows = x_refs[0].shape[0]
    tokens = jnp.concatenate([x[:, :features] for x in x_refs], axis=0)
    gates = jnp.concatenate([x[:, features:] for x in x_refs], axis=0).astype(jnp.float32)
    lane = lax.broadcasted_iota(jnp.int32, gates.shape, 1)
    local, rank = up_own_ref.shape[:2]
    shared = jnp.dot(tokens, base_ref[...], preferred_element_type=jnp.float32)
    latent = jnp.dot(tokens, down_ref[...], preferred_element_type=jnp.float32)
    latent = latent.astype(jnp.bfloat16)
    total = jnp.zeros_like(shared)
    for j in range(2 * local):
        up = up_own_ref[j] if j < local else up_peer_ref[j - local]
        change = jnp.dot(
            latent[:, j * rank : (j + 1) * rank], up, preferred_element_type=jnp.float32
        )
        value = shared + change.astype(jnp.bfloat16).astype(jnp.float32)
        hidden = (value / (1.0 + jnp.exp(-value))).astype(jnp.bfloat16).astype(jnp.float32)
        expert = first_ref[j // local] + j % local
        gate = jnp.sum(jnp.where(lane == expert, gates, 0.0), axis=1, keepdims=True)
        total = total + gate * hidden
    for b, out_ref in enumerate(out_refs):
        out_ref[...] = total[b * rows : (b + 1) * rows].astype(out_ref.dtype)


def sum_body(*refs):
    total = refs[0][...].astype(jnp.float32)
    for ref in refs[1:-1]:
        total = total + ref[...].astype(jnp.float32)
    refs[-1][...] = total.astype(refs[-1].dtype)


def shards(tokens, routes, gate_code, base_weight, delta_in, delta_out):
    devices_count = lax.axis_size("expert")
    me = lax.axis_index("expert")
    local, features, rank = delta_in.shape
    rows = tokens.shape[0]
    hidden_units = base_weight.shape[1]
    experts = local * devices_count
    width = -(-experts // lanes) * lanes
    chips = devices_count // 2
    minor = 1 << ((chips.bit_length() - 1) // 2)

    def exchange(value, mask):
        return lax.ppermute(value, "expert", [(i, i ^ mask) for i in range(devices_count)])

    packed = pl.pallas_call(
        pack_body,
        out_shape=jax.ShapeDtypeStruct((rows, features + width), tokens.dtype),
        in_specs=[vmem] * 3,
        out_specs=vmem,
        cost_estimate=pl.CostEstimate(flops=0, bytes_accessed=500000, transcendentals=0),
    )(tokens, routes, gate_code)
    down_peer, up_peer = exchange(delta_in, 1), exchange(delta_out, 1)
    down = jnp.concatenate([*delta_in, *down_peer], axis=1)
    first = jnp.stack([me, me ^ 1]).astype(jnp.int32) * local

    def experts_on(blocks):
        count = len(blocks)
        return pl.pallas_call(
            functools.partial(expert_body, features, count),
            out_shape=[jax.ShapeDtypeStruct((rows, hidden_units), jnp.bfloat16)] * count,
            in_specs=[pl.BlockSpec(memory_space=pltpu.SMEM)] + [vmem] * (count + 4),
            out_specs=[vmem] * count,
            compiler_params=pltpu.CompilerParams(vmem_limit_bytes=36 << 20),
            cost_estimate=pl.CostEstimate(
                flops=2 * rows * count * features * (hidden_units + 2 * local * rank),
                bytes_accessed=9000000,
                transcendentals=0,
            ),
        )(first, *blocks, base_weight, down, delta_out, up_peer)

    majors = range(0, chips, minor)
    column = [packed if m == 0 else exchange(packed, 2 * m) for m in majors]
    partial = []
    for n in range(minor):
        held = column if n == 0 else [exchange(block, 2 * n) for block in column]
        for m, part in zip(majors, experts_on(held)):
            mask = 2 * (m + n)
            partial.append(part if mask == 0 else exchange(part, mask))
    return pl.pallas_call(
        sum_body,
        out_shape=jax.ShapeDtypeStruct((rows, hidden_units), jnp.bfloat16),
        in_specs=[vmem] * chips,
        out_specs=vmem,
    )(*partial)


def solution(mesh):
    placed = (
        P(("groups", "expert"), None),
        P(("groups", "expert"), None),
        P(("groups", "expert"), None),
        P(),
        P("expert", None, None),
        P("expert", None, None),
    )
    return jax.shard_map(
        shards, mesh=mesh, in_specs=placed, out_specs=P(("groups", "expert"), None), check_vma=False
    )
```

```python
import functools
import jax
import jax.numpy as jnp
from jax import lax
from jax.experimental import pallas as pl
from jax.experimental.pallas import tpu as pltpu
from jax.sharding import PartitionSpec as P

gate_levels = 16.0
lanes = 128
most = 8
vmem = pl.BlockSpec(memory_space=pltpu.VMEM)


def pack_body(tokens_ref, routes_ref, codes_ref, out_ref, routes_buf, codes_buf, sems):
    rows, features = tokens_ref.shape
    width = out_ref.shape[1] - features
    copies = [
        pltpu.make_async_copy(routes_ref, routes_buf, sems.at[0]),
        pltpu.make_async_copy(codes_ref, codes_buf, sems.at[1]),
        pltpu.make_async_copy(tokens_ref, out_ref.at[:, pl.ds(0, features)], sems.at[2]),
    ]
    for copy in copies:
        copy.start()
    copies[0].wait()
    copies[1].wait()
    lane = lax.broadcasted_iota(jnp.int32, (rows, width), 1)
    routes = routes_buf[...].T
    weights = (codes_buf[...].astype(jnp.float32).T + 1.0) / gate_levels
    gates = jnp.zeros((rows, width), jnp.float32)
    for k in range(routes.shape[1]):
        gates = gates + jnp.where(routes[:, k : k + 1] == lane, weights[:, k : k + 1], 0.0)
    out_ref[:, features:] = gates.astype(out_ref.dtype)
    copies[2].wait()


def weave_body(own_ref, peer_ref, out_ref):
    local, _, rank = own_ref.shape
    for j in range(local):
        out_ref[:, j * rank : (j + 1) * rank] = own_ref[j]
        out_ref[:, (local + j) * rank : (local + j + 1) * rank] = peer_ref[j]


def expert_body(features, blocks, *refs):
    x_refs = refs[:blocks]
    base_ref, down_ref, up_own_ref, up_peer_ref = refs[blocks : 4 + blocks]
    out_refs = refs[4 + blocks :]
    me = lax.axis_index("expert")
    rows = x_refs[0].shape[0]
    tokens = jnp.concatenate([x[:, :features] for x in x_refs], axis=0)
    gates = jnp.concatenate([x[:, features:] for x in x_refs], axis=0).astype(jnp.float32)
    lane = lax.broadcasted_iota(jnp.int32, gates.shape, 1)
    local, rank = up_own_ref.shape[:2]
    shared = jnp.dot(tokens, base_ref[...], preferred_element_type=jnp.float32)
    latent = jnp.dot(tokens, down_ref[...], preferred_element_type=jnp.float32)
    latent = latent.astype(jnp.bfloat16)
    total = jnp.zeros_like(shared)
    for j in range(2 * local):
        up = up_own_ref[j] if j < local else up_peer_ref[j - local]
        change = jnp.dot(
            latent[:, j * rank : (j + 1) * rank], up, preferred_element_type=jnp.float32
        )
        value = shared + change.astype(jnp.bfloat16).astype(jnp.float32)
        hidden = (value / (1.0 + jnp.exp(-value))).astype(jnp.bfloat16).astype(jnp.float32)
        expert = (me if j < local else me ^ 1) * local + j % local
        gate = jnp.sum(jnp.where(lane == expert, gates, 0.0), axis=1, keepdims=True)
        total = total + gate * hidden
    for b, out_ref in enumerate(out_refs):
        out_ref[...] = total[b * rows : (b + 1) * rows].astype(out_ref.dtype)


def sum_body(*refs):
    total = refs[0][...].astype(jnp.float32)
    for ref in refs[1:-1]:
        total = total + ref[...].astype(jnp.float32)
    refs[-1][...] = total.astype(refs[-1].dtype)


def shards(tokens, routes, gate_code, base_weight, delta_in, delta_out):
    devices_count = lax.axis_size("expert")
    local, features, rank = delta_in.shape
    rows = tokens.shape[0]
    hidden_units = base_weight.shape[1]
    experts = local * devices_count
    width = -(-experts // lanes) * lanes
    chips = devices_count // 2
    minor = 1 << ((chips.bit_length() - 1) // 2)

    def exchange(value, mask):
        return lax.ppermute(value, "expert", [(i, i ^ mask) for i in range(devices_count)])

    def small(body, shape, count, megabytes, moved):
        return pl.pallas_call(
            body,
            out_shape=jax.ShapeDtypeStruct(shape, jnp.bfloat16),
            in_specs=[vmem] * count,
            out_specs=vmem,
            compiler_params=pltpu.CompilerParams(vmem_limit_bytes=megabytes << 20),
            cost_estimate=pl.CostEstimate(flops=0, bytes_accessed=moved, transcendentals=0),
        )

    def experts_on(blocks):
        count = len(blocks)
        return pl.pallas_call(
            functools.partial(expert_body, features, count),
            out_shape=[jax.ShapeDtypeStruct((rows, hidden_units), jnp.bfloat16)] * count,
            in_specs=[vmem] * (count + 4),
            out_specs=[vmem] * count,
            compiler_params=pltpu.CompilerParams(vmem_limit_bytes=26 << 20),
            cost_estimate=pl.CostEstimate(
                flops=2 * rows * count * features * (hidden_units + 2 * local * rank),
                bytes_accessed=9000000,
                transcendentals=0,
            ),
        )(*blocks, base_weight, down, delta_out, up_peer)

    down_peer, up_peer = exchange(delta_in, 1), exchange(delta_out, 1)
    packed = pl.pallas_call(
        pack_body,
        out_shape=jax.ShapeDtypeStruct((rows, features + width), tokens.dtype),
        in_specs=[pl.BlockSpec(memory_space=pltpu.HBM)] * 3,
        out_specs=vmem,
        scratch_shapes=[
            pltpu.VMEM(routes.shape[::-1], jnp.int32),
            pltpu.VMEM(routes.shape[::-1], jnp.int32),
            pltpu.SemaphoreType.DMA((3,)),
        ],
        compiler_params=pltpu.CompilerParams(vmem_limit_bytes=4 << 20),
        cost_estimate=pl.CostEstimate(flops=0, bytes_accessed=2000000, transcendentals=0),
    )(tokens, routes.T, gate_code.T)
    down = small(weave_body, (features, 2 * local * rank), 2, 9, 4000000)(delta_in, down_peer)

    held = {0: packed}
    partial = list(experts_on([packed]))
    for stage in range(1, chips.bit_length()):
        if stage == 2:
            firsts = [m for m in held if m]
            *blocks, partial[0] = lax.optimization_barrier([*(held[m] for m in firsts), partial[0]])
            held.update(zip(firsts, blocks))
        for m in range(chips):
            if m.bit_count() == stage:
                high = m & -minor
                rest = m if high == m or high.bit_count() > 1 else m ^ high
                hop = rest & -rest
                if high.bit_count() > 1:
                    hop = high & -high
                held[m] = exchange(held[m ^ hop], 2 * hop)
    for stage in range(1, chips.bit_length()):
        masks = [m for m in range(chips) if m.bit_count() == stage]
        for at in range(0, len(masks), most):
            some = masks[at : at + most]
            for m, part in zip(some, experts_on([held[m] for m in some])):
                partial.append(exchange(part, 2 * m))
    return small(sum_body, (rows, hidden_units), chips, 8, 2000000)(*partial)


def solution(mesh):
    placed = (
        P(("groups", "expert"), None),
        P(("groups", "expert"), None),
        P(("groups", "expert"), None),
        P(),
        P("expert", None, None),
        P("expert", None, None),
    )
    return jax.shard_map(
        shards, mesh=mesh, in_specs=placed, out_specs=P(("groups", "expert"), None), check_vma=False
    )
```

```python
import functools
import jax
import jax.numpy as jnp
from jax import lax
from jax.experimental import pallas as pl
from jax.experimental.pallas import tpu as pltpu
from jax.sharding import PartitionSpec as P

levels = 16
lanes = 128
most = 8
vmem = pl.BlockSpec(memory_space=pltpu.VMEM)


def pack_body(tokens_ref, marks_ref, out_ref):
    rows, features = tokens_ref.shape
    width = out_ref.shape[1] - features
    out_ref[:, :features] = tokens_ref[...]
    lane = lax.broadcasted_iota(jnp.int32, (rows, width), 1)
    marks = marks_ref[...].T
    routes = marks // levels
    weights = (marks % levels + 1).astype(jnp.float32) / levels
    gates = jnp.zeros((rows, width), jnp.float32)
    for k in range(marks.shape[1]):
        gates = gates + jnp.where(routes[:, k : k + 1] == lane, weights[:, k : k + 1], 0.0)
    out_ref[:, features:] = gates.astype(out_ref.dtype)


def weave_body(own_ref, peer_ref, out_ref):
    local, _, rank = own_ref.shape
    for j in range(local):
        out_ref[:, j * rank : (j + 1) * rank] = own_ref[j]
        out_ref[:, (local + j) * rank : (local + j + 1) * rank] = peer_ref[j]


def expert_body(features, blocks, *refs):
    x_refs = refs[:blocks]
    base_ref, down_ref, up_own_ref, up_peer_ref = refs[blocks : 4 + blocks]
    out_refs = refs[4 + blocks :]
    me = lax.axis_index("expert")
    rows = x_refs[0].shape[0]
    tokens = jnp.concatenate([x[:, :features] for x in x_refs], axis=0)
    gates = jnp.concatenate([x[:, features:] for x in x_refs], axis=0).astype(jnp.float32)
    lane = lax.broadcasted_iota(jnp.int32, gates.shape, 1)
    local, rank = up_own_ref.shape[:2]
    shared = jnp.dot(tokens, base_ref[...], preferred_element_type=jnp.float32)
    latent = jnp.dot(tokens, down_ref[...], preferred_element_type=jnp.float32)
    latent = latent.astype(jnp.bfloat16)
    total = jnp.zeros_like(shared)
    for j in range(2 * local):
        up = up_own_ref[j] if j < local else up_peer_ref[j - local]
        change = jnp.dot(
            latent[:, j * rank : (j + 1) * rank], up, preferred_element_type=jnp.float32
        )
        value = shared + change.astype(jnp.bfloat16).astype(jnp.float32)
        hidden = (value / (1.0 + jnp.exp(-value))).astype(jnp.bfloat16).astype(jnp.float32)
        expert = (me if j < local else me ^ 1) * local + j % local
        gate = jnp.sum(jnp.where(lane == expert, gates, 0.0), axis=1, keepdims=True)
        total = total + gate * hidden
    for b, out_ref in enumerate(out_refs):
        out_ref[...] = total[b * rows : (b + 1) * rows].astype(out_ref.dtype)


def sum_body(*refs):
    total = refs[0][...].astype(jnp.float32)
    for ref in refs[1:-1]:
        total = total + ref[...].astype(jnp.float32)
    refs[-1][...] = total.astype(refs[-1].dtype)


def shards(tokens, routes, gate_code, base_weight, delta_in, delta_out):
    devices_count = lax.axis_size("expert")
    local, features, rank = delta_in.shape
    rows = tokens.shape[0]
    hidden_units = base_weight.shape[1]
    experts = local * devices_count
    width = -(-experts // lanes) * lanes
    chips = devices_count // 2
    minor = 1 << ((chips.bit_length() - 1) // 2)

    def exchange(value, mask):
        return lax.ppermute(value, "expert", [(i, i ^ mask) for i in range(devices_count)])

    def small(body, shape, count, megabytes, moved):
        return pl.pallas_call(
            body,
            out_shape=jax.ShapeDtypeStruct(shape, jnp.bfloat16),
            in_specs=[vmem] * count,
            out_specs=vmem,
            compiler_params=pltpu.CompilerParams(vmem_limit_bytes=megabytes << 20),
            cost_estimate=pl.CostEstimate(flops=0, bytes_accessed=moved, transcendentals=0),
        )

    def experts_on(blocks):
        count = len(blocks)
        return pl.pallas_call(
            functools.partial(expert_body, features, count),
            out_shape=[jax.ShapeDtypeStruct((rows, hidden_units), jnp.bfloat16)] * count,
            in_specs=[vmem] * (count + 4),
            out_specs=[vmem] * count,
            compiler_params=pltpu.CompilerParams(vmem_limit_bytes=26 << 20),
            cost_estimate=pl.CostEstimate(
                flops=2 * rows * count * features * (hidden_units + 2 * local * rank),
                bytes_accessed=9000000,
                transcendentals=0,
            ),
        )(*blocks, base_weight, down, delta_out, up_peer)

    down_peer, up_peer = exchange(delta_in, 1), exchange(delta_out, 1)
    marks = routes.T * levels + gate_code.T
    packed = small(pack_body, (rows, features + width), 2, 4, 2000000)(tokens, marks)
    down = small(weave_body, (features, 2 * local * rank), 2, 9, 4000000)(delta_in, down_peer)

    stages = chips.bit_length()
    of = [[m for m in range(chips - 1, -1, -1) if m.bit_count() == s] for s in range(stages)]

    def hop_of(m):
        high = m & -minor
        rest = high if high == m or high.bit_count() > 1 else m ^ high
        return rest & -rest

    held, parts, home = {0: packed}, {}, {}

    def tie(*stores):
        keys = [(store, m) for store, masks in stores for m in masks]
        for (store, m), value in zip(keys, lax.optimization_barrier([s[m] for s, m in keys])):
            store[m] = value

    def compute(masks):
        for at in range(0, len(masks), most):
            some = masks[at : at + most]
            parts.update(zip(some, experts_on([held[m] for m in some])))

    def send_home(masks):
        home.update((m, exchange(parts[m], 2 * m) if m else parts[m]) for m in masks)

    for stage in range(1, stages):
        sources = sorted({m ^ hop_of(m) for m in of[stage]}, reverse=True)
        if stage >= 2:
            tie((held, sources), (parts, of[stage - 2]))
            send_home(of[stage - 2])
        for m in of[stage]:
            held[m] = exchange(held[m ^ hop_of(m)], 2 * hop_of(m))
        compute(of[stage - 1])
    tie((held, of[-1]), (home, of[-3]), (parts, of[-2]))
    compute(of[-1])
    tie((parts, of[-2] + of[-1]))
    send_home(of[-2] + of[-1])
    partial = list(home.values())
    return small(sum_body, (rows, hidden_units), chips, 8, 2000000)(*partial)


def solution(mesh):
    placed = (
        P(("groups", "expert"), None),
        P(("groups", "expert"), None),
        P(("groups", "expert"), None),
        P(),
        P("expert", None, None),
        P("expert", None, None),
    )
    return jax.shard_map(
        shards, mesh=mesh, in_specs=placed, out_specs=P(("groups", "expert"), None), check_vma=False
    )
```

```python
import functools
import jax
import jax.numpy as jnp
from jax import lax
from jax.experimental import pallas as pl
from jax.experimental.pallas import tpu as pltpu
from jax.sharding import PartitionSpec as P

levels = 16
lanes = 128
most = 8
vmem = pl.BlockSpec(memory_space=pltpu.VMEM)


def pack_body(tokens_ref, marks_ref, out_ref):
    rows, features = tokens_ref.shape
    width = out_ref.shape[1] - features
    out_ref[:, :features] = tokens_ref[...]
    lane = lax.broadcasted_iota(jnp.int32, (rows, width), 1)
    marks = marks_ref[...].T
    routes = marks // levels
    weights = (marks % levels + 1).astype(jnp.float32) / levels
    gates = jnp.zeros((rows, width), jnp.float32)
    for k in range(marks.shape[1]):
        gates = gates + jnp.where(routes[:, k : k + 1] == lane, weights[:, k : k + 1], 0.0)
    out_ref[:, features:] = gates.astype(out_ref.dtype)


def weave_body(own_ref, peer_ref, out_ref):
    local, _, rank = own_ref.shape
    for j in range(local):
        out_ref[:, j * rank : (j + 1) * rank] = own_ref[j]
        out_ref[:, (local + j) * rank : (local + j + 1) * rank] = peer_ref[j]


def expert_body(features, blocks, *refs):
    x_refs = refs[:blocks]
    base_ref, down_ref, up_own_ref, up_peer_ref = refs[blocks : 4 + blocks]
    out_refs = refs[4 + blocks :]
    me = lax.axis_index("expert")
    rows = x_refs[0].shape[0]
    tokens = jnp.concatenate([x[:, :features] for x in x_refs], axis=0)
    gates = jnp.concatenate([x[:, features:] for x in x_refs], axis=0).astype(jnp.float32)
    lane = lax.broadcasted_iota(jnp.int32, gates.shape, 1)
    local, rank = up_own_ref.shape[:2]
    shared = jnp.dot(tokens, base_ref[...], preferred_element_type=jnp.float32)
    latent = jnp.dot(tokens, down_ref[...], preferred_element_type=jnp.float32)
    latent = latent.astype(jnp.bfloat16)
    total = jnp.zeros_like(shared)
    for j in range(2 * local):
        up = up_own_ref[j] if j < local else up_peer_ref[j - local]
        change = jnp.dot(
            latent[:, j * rank : (j + 1) * rank], up, preferred_element_type=jnp.float32
        )
        value = shared + change.astype(jnp.bfloat16).astype(jnp.float32)
        hidden = (value / (1.0 + jnp.exp(-value))).astype(jnp.bfloat16).astype(jnp.float32)
        expert = (me if j < local else me ^ 1) * local + j % local
        gate = jnp.sum(jnp.where(lane == expert, gates, 0.0), axis=1, keepdims=True)
        total = total + gate * hidden
    for b, out_ref in enumerate(out_refs):
        out_ref[...] = total[b * rows : (b + 1) * rows].astype(out_ref.dtype)


def sum_body(*refs):
    total = refs[0][...].astype(jnp.float32)
    for ref in refs[1:-1]:
        total = total + ref[...].astype(jnp.float32)
    refs[-1][...] = total.astype(refs[-1].dtype)


def shards(tokens, routes, gate_code, base_weight, delta_in, delta_out):
    devices_count = lax.axis_size("expert")
    local, features, rank = delta_in.shape
    rows = tokens.shape[0]
    hidden_units = base_weight.shape[1]
    experts = local * devices_count
    width = -(-experts // lanes) * lanes
    chips = devices_count // 2
    minor = 1 << ((chips.bit_length() - 1) // 2)

    def exchange(value, mask):
        return lax.ppermute(value, "expert", [(i, i ^ mask) for i in range(devices_count)])

    def small(body, shape, count, megabytes, moved):
        return pl.pallas_call(
            body,
            out_shape=jax.ShapeDtypeStruct(shape, jnp.bfloat16),
            in_specs=[vmem] * count,
            out_specs=vmem,
            compiler_params=pltpu.CompilerParams(vmem_limit_bytes=megabytes << 20),
            cost_estimate=pl.CostEstimate(flops=0, bytes_accessed=moved, transcendentals=0),
        )

    def experts_on(blocks):
        count = len(blocks)
        return pl.pallas_call(
            functools.partial(expert_body, features, count),
            out_shape=[jax.ShapeDtypeStruct((rows, hidden_units), jnp.bfloat16)] * count,
            in_specs=[vmem] * (count + 4),
            out_specs=[vmem] * count,
            compiler_params=pltpu.CompilerParams(vmem_limit_bytes=26 << 20),
            cost_estimate=pl.CostEstimate(
                flops=2 * rows * count * features * (hidden_units + 2 * local * rank),
                bytes_accessed=9000000,
                transcendentals=0,
            ),
        )(*blocks, base_weight, down, delta_out, up_peer)

    down_peer, up_peer = exchange(delta_in, 1), exchange(delta_out, 1)
    marks = routes.T * levels + gate_code.T
    packed = small(pack_body, (rows, features + width), 2, 4, 2000000)(tokens, marks)
    down = small(weave_body, (features, 2 * local * rank), 2, 9, 4000000)(delta_in, down_peer)

    def hop_of(m):
        major, low = m & -minor, m & (minor - 1)
        if major and low:
            return low if major.bit_count() == 1 else major
        return m & -m

    def depth(m):
        return 1 + depth(m ^ hop_of(m)) if m else 0

    stages = 1 + max(depth(m) for m in range(chips))
    of = [[m for m in range(chips - 1, -1, -1) if depth(m) == s] for s in range(stages)]

    held, parts, home = {0: packed}, {}, {}

    def tie(*stores):
        keys = [(store, m) for store, masks in stores for m in masks]
        for (store, m), value in zip(keys, lax.optimization_barrier([s[m] for s, m in keys])):
            store[m] = value

    def compute(masks):
        for at in range(0, len(masks), most):
            some = masks[at : at + most]
            parts.update(zip(some, experts_on([held[m] for m in some])))

    def send_home(masks):
        home.update((m, exchange(parts[m], 2 * m) if m else parts[m]) for m in masks)

    def fetch(masks):
        for m in masks:
            held[m] = exchange(held[m ^ hop_of(m)], 2 * hop_of(m))

    fetch(of[1])
    near = of[1][-1]
    held[near], down = lax.optimization_barrier((held[near], down))
    compute(of[0])
    send_home(of[0])
    crossing = [m for m in of[2] if hop_of(m) >= minor and m & (minor - 1)]
    fetch(crossing)
    tie((held, [m for m in of[1] if m >= minor]), (parts, of[0]))
    fetch([m for m in of[2] if m not in crossing])
    compute(of[1])
    send_home(of[1])
    for stage in range(3, stages):
        fetch(of[stage])
        compute(of[stage - 1])
        send_home(of[stage - 1])
    last = sorted(of[-1], key=lambda m: (m not in crossing, hop_of(m) >= minor, -m))
    compute(last)
    send_home(last)
    partial = list(home.values())
    return small(sum_body, (rows, hidden_units), chips, 8, 2000000)(*partial)


def solution(mesh):
    placed = (
        P(("groups", "expert"), None),
        P(("groups", "expert"), None),
        P(("groups", "expert"), None),
        P(),
        P("expert", None, None),
        P("expert", None, None),
    )
    return jax.shard_map(
        shards, mesh=mesh, in_specs=placed, out_specs=P(("groups", "expert"), None), check_vma=False
    )
```

```python
import functools
import jax
import jax.numpy as jnp
from jax import lax
from jax.experimental import pallas as pl
from jax.experimental.pallas import tpu as pltpu
from jax.sharding import PartitionSpec as P

levels = 16
lanes = 128
most = 8
vmem = pl.BlockSpec(memory_space=pltpu.VMEM)


def pack_body(tokens_ref, marks_ref, out_ref):
    rows, features = tokens_ref.shape
    width = out_ref.shape[1] - features
    out_ref[:, :features] = tokens_ref[...]
    lane = lax.broadcasted_iota(jnp.int32, (rows, width), 1)
    marks = marks_ref[...].T
    routes = marks // levels
    weights = (marks % levels + 1).astype(jnp.float32) / levels
    gates = jnp.zeros((rows, width), jnp.float32)
    for k in range(marks.shape[1]):
        gates = gates + jnp.where(routes[:, k : k + 1] == lane, weights[:, k : k + 1], 0.0)
    out_ref[:, features:] = gates.astype(out_ref.dtype)


def weave_body(own_ref, peer_ref, out_ref):
    local, _, rank = own_ref.shape
    for j in range(local):
        out_ref[:, j * rank : (j + 1) * rank] = own_ref[j]
        out_ref[:, (local + j) * rank : (local + j + 1) * rank] = peer_ref[j]


def expert_body(features, blocks, *refs):
    x_refs = refs[:blocks]
    base_ref, down_ref, up_own_ref, up_peer_ref = refs[blocks : 4 + blocks]
    out_refs = refs[4 + blocks :]
    me = lax.axis_index("expert")
    rows = x_refs[0].shape[0]
    tokens = jnp.concatenate([x[:, :features] for x in x_refs], axis=0)
    gates = jnp.concatenate([x[:, features:] for x in x_refs], axis=0).astype(jnp.float32)
    lane = lax.broadcasted_iota(jnp.int32, gates.shape, 1)
    local, rank = up_own_ref.shape[:2]
    shared = jnp.dot(tokens, base_ref[...], preferred_element_type=jnp.float32)
    latent = jnp.dot(tokens, down_ref[...], preferred_element_type=jnp.float32)
    latent = latent.astype(jnp.bfloat16)
    total = jnp.zeros_like(shared)
    for j in range(2 * local):
        up = up_own_ref[j] if j < local else up_peer_ref[j - local]
        change = jnp.dot(
            latent[:, j * rank : (j + 1) * rank], up, preferred_element_type=jnp.float32
        )
        value = shared + change.astype(jnp.bfloat16).astype(jnp.float32)
        hidden = (value / (1.0 + jnp.exp(-value))).astype(jnp.bfloat16).astype(jnp.float32)
        expert = (me if j < local else me ^ 1) * local + j % local
        gate = jnp.sum(jnp.where(lane == expert, gates, 0.0), axis=1, keepdims=True)
        total = total + gate * hidden
    for b, out_ref in enumerate(out_refs):
        out_ref[...] = total[b * rows : (b + 1) * rows].astype(out_ref.dtype)


def sum_body(*refs):
    total = refs[0][...].astype(jnp.float32)
    for ref in refs[1:-1]:
        total = total + ref[...].astype(jnp.float32)
    refs[-1][...] = total.astype(refs[-1].dtype)


def shards(tokens, routes, gate_code, base_weight, delta_in, delta_out):
    devices_count = lax.axis_size("expert")
    local, features, rank = delta_in.shape
    rows = tokens.shape[0]
    hidden_units = base_weight.shape[1]
    experts = local * devices_count
    width = -(-experts // lanes) * lanes
    chips = devices_count // 2
    minor = 1 << ((chips.bit_length() - 1) // 2)

    def exchange(value, mask):
        return lax.ppermute(value, "expert", [(i, i ^ mask) for i in range(devices_count)])

    def small(body, shape, count, megabytes, moved):
        return pl.pallas_call(
            body,
            out_shape=jax.ShapeDtypeStruct(shape, jnp.bfloat16),
            in_specs=[vmem] * count,
            out_specs=vmem,
            compiler_params=pltpu.CompilerParams(vmem_limit_bytes=megabytes << 20),
            cost_estimate=pl.CostEstimate(flops=0, bytes_accessed=moved, transcendentals=0),
        )

    def experts_on(blocks):
        count = len(blocks)
        return pl.pallas_call(
            functools.partial(expert_body, features, count),
            out_shape=[jax.ShapeDtypeStruct((rows, hidden_units), jnp.bfloat16)] * count,
            in_specs=[vmem] * (count + 4),
            out_specs=[vmem] * count,
            compiler_params=pltpu.CompilerParams(vmem_limit_bytes=26 << 20),
            cost_estimate=pl.CostEstimate(
                flops=2 * rows * count * features * (hidden_units + 2 * local * rank),
                bytes_accessed=9000000,
                transcendentals=0,
            ),
        )(*blocks, base_weight, down, delta_out, up_peer)

    down_peer, up_peer = exchange(delta_in, 1), exchange(delta_out, 1)
    marks = routes.T * levels + gate_code.T
    packed = small(pack_body, (rows, features + width), 2, 4, 2000000)(tokens, marks)
    down = small(weave_body, (features, 2 * local * rank), 2, 9, 4000000)(delta_in, down_peer)

    def hop_of(m):
        major, low = m & -minor, m & (minor - 1)
        if major and low:
            return low if major.bit_count() == 1 else major
        return m & -m

    def depth(m):
        return 1 + depth(m ^ hop_of(m)) if m else 0

    stages = 1 + max(depth(m) for m in range(chips))
    of = [[m for m in range(chips - 1, -1, -1) if depth(m) == s] for s in range(stages)]

    held, parts, home = {0: packed}, {}, {}

    def tie(*stores):
        keys = [(store, m) for store, masks in stores for m in masks]
        for (store, m), value in zip(keys, lax.optimization_barrier([s[m] for s, m in keys])):
            store[m] = value

    def compute(masks):
        for at in range(0, len(masks), most):
            some = masks[at : at + most]
            parts.update(zip(some, experts_on([held[m] for m in some])))

    def send_home(masks):
        home.update((m, exchange(parts[m], 2 * m) if m else parts[m]) for m in masks)

    def fetch(masks):
        for m in masks:
            held[m] = exchange(held[m ^ hop_of(m)], 2 * hop_of(m))

    fetch(of[1])
    near = of[1][-1]
    held[near], down = lax.optimization_barrier((held[near], down))
    compute(of[0])
    send_home(of[0])
    crossing = [m for m in of[2] if hop_of(m) >= minor and m & (minor - 1)]
    fetch(crossing)
    tie((held, [m for m in of[1] if m >= minor]), (parts, of[0]))
    fetch([m for m in of[2] if m not in crossing])
    first = sorted(of[1], key=lambda m: (m < minor, m))
    compute(first)
    send_home(of[1])
    for stage in range(3, stages):
        fetch(of[stage])
        compute(of[stage - 1])
        send_home(of[stage - 1])
    last = sorted(of[-1], key=lambda m: (m not in crossing, hop_of(m) >= minor, -m))
    compute(last)
    send_home([m for m in last if m >= 2 * minor] + [m for m in last if m < 2 * minor])
    partial = list(home.values())
    return small(sum_body, (rows, hidden_units), chips, 8, 2000000)(*partial)


def solution(mesh):
    placed = (
        P(("groups", "expert"), None),
        P(("groups", "expert"), None),
        P(("groups", "expert"), None),
        P(),
        P("expert", None, None),
        P("expert", None, None),
    )
    return jax.shard_map(
        shards, mesh=mesh, in_specs=placed, out_specs=P(("groups", "expert"), None), check_vma=False
    )
```

```python
import functools
import jax
import jax.numpy as jnp
from jax import lax
from jax.experimental import pallas as pl
from jax.experimental.pallas import tpu as pltpu
from jax.sharding import PartitionSpec as P

levels = 16
lanes = 128
most = 8
anywhere = pl.BlockSpec(memory_space=pl.ANY)
vmem = pl.BlockSpec(memory_space=pltpu.VMEM)


def pack_body(tokens_ref, marks_ref, out_ref):
    rows, features = tokens_ref.shape
    width = out_ref.shape[1] - features
    out_ref[:, :features] = tokens_ref[...]
    lane = lax.broadcasted_iota(jnp.int32, (rows, width), 1)
    marks = marks_ref[...].T
    routes = marks // levels
    weights = (marks % levels + 1).astype(jnp.float32) / levels
    gates = jnp.zeros((rows, width), jnp.float32)
    for k in range(marks.shape[1]):
        gates = gates + jnp.where(routes[:, k : k + 1] == lane, weights[:, k : k + 1], 0.0)
    out_ref[:, features:] = gates.astype(out_ref.dtype)


def weave_body(own_ref, peer_ref, out_ref):
    local, _, rank = own_ref.shape
    for j in range(local):
        out_ref[:, j * rank : (j + 1) * rank] = own_ref[j]
        out_ref[:, (local + j) * rank : (local + j + 1) * rank] = peer_ref[j]


def gate_body(after_ref, block_ref, out_ref):
    del after_ref, block_ref, out_ref


def expert_body(features, blocks, *refs):
    x_refs = refs[:blocks]
    base_ref, down_ref, up_own_ref, up_peer_ref = refs[blocks : 4 + blocks]
    out_refs = refs[4 + blocks :]
    me = lax.axis_index("expert")
    rows = x_refs[0].shape[0]
    tokens = jnp.concatenate([x[:, :features] for x in x_refs], axis=0)
    gates = jnp.concatenate([x[:, features:] for x in x_refs], axis=0).astype(jnp.float32)
    lane = lax.broadcasted_iota(jnp.int32, gates.shape, 1)
    local, rank = up_own_ref.shape[:2]
    shared = jnp.dot(tokens, base_ref[...], preferred_element_type=jnp.float32)
    latent = jnp.dot(tokens, down_ref[...], preferred_element_type=jnp.float32)
    latent = latent.astype(jnp.bfloat16)
    total = jnp.zeros_like(shared)
    for j in range(2 * local):
        up = up_own_ref[j] if j < local else up_peer_ref[j - local]
        change = jnp.dot(
            latent[:, j * rank : (j + 1) * rank], up, preferred_element_type=jnp.float32
        )
        value = shared + change.astype(jnp.bfloat16).astype(jnp.float32)
        hidden = (value / (1.0 + jnp.exp(-value))).astype(jnp.bfloat16).astype(jnp.float32)
        expert = (me if j < local else me ^ 1) * local + j % local
        gate = jnp.sum(jnp.where(lane == expert, gates, 0.0), axis=1, keepdims=True)
        total = total + gate * hidden
    for b, out_ref in enumerate(out_refs):
        out_ref[...] = total[b * rows : (b + 1) * rows].astype(out_ref.dtype)


def sum_body(*refs):
    total = refs[0][...].astype(jnp.float32)
    for ref in refs[1:-1]:
        total = total + ref[...].astype(jnp.float32)
    refs[-1][...] = total.astype(refs[-1].dtype)


def shards(tokens, routes, gate_code, base_weight, delta_in, delta_out):
    devices_count = lax.axis_size("expert")
    local, features, rank = delta_in.shape
    rows = tokens.shape[0]
    hidden_units = base_weight.shape[1]
    experts = local * devices_count
    width = -(-experts // lanes) * lanes
    chips = devices_count // 2
    minor = 1 << ((chips.bit_length() - 1) // 2)

    def exchange(value, mask):
        return lax.ppermute(value, "expert", [(i, i ^ mask) for i in range(devices_count)])

    def small(body, shape, count, megabytes, moved):
        return pl.pallas_call(
            body,
            out_shape=jax.ShapeDtypeStruct(shape, jnp.bfloat16),
            in_specs=[vmem] * count,
            out_specs=vmem,
            compiler_params=pltpu.CompilerParams(vmem_limit_bytes=megabytes << 20),
            cost_estimate=pl.CostEstimate(flops=0, bytes_accessed=moved, transcendentals=0),
        )

    def experts_on(blocks):
        count = len(blocks)
        return pl.pallas_call(
            functools.partial(expert_body, features, count),
            out_shape=[jax.ShapeDtypeStruct((rows, hidden_units), jnp.bfloat16)] * count,
            in_specs=[vmem] * (count + 4),
            out_specs=[vmem] * count,
            compiler_params=pltpu.CompilerParams(vmem_limit_bytes=26 << 20),
            cost_estimate=pl.CostEstimate(
                flops=2 * rows * count * features * (hidden_units + 2 * local * rank),
                bytes_accessed=9000000,
                transcendentals=0,
            ),
        )(*blocks, base_weight, down, delta_out, up_peer)

    down_peer, up_peer = exchange(delta_in, 1), exchange(delta_out, 1)
    marks = routes.T * levels + gate_code.T
    packed = small(pack_body, (rows, features + width), 2, 4, 2000000)(tokens, marks)
    down = small(weave_body, (features, 2 * local * rank), 2, 9, 4000000)(delta_in, down_peer)

    def hop_of(m):
        major, low = m & -minor, m & (minor - 1)
        if major and low:
            return low if major.bit_count() == 1 else major
        return m & -m

    def depth(m):
        return 1 + depth(m ^ hop_of(m)) if m else 0

    stages = 1 + max(depth(m) for m in range(chips))
    of = [[m for m in range(chips - 1, -1, -1) if depth(m) == s] for s in range(stages)]

    held, parts, home = {0: packed}, {}, {}

    def tie(*stores):
        keys = [(store, m) for store, masks in stores for m in masks]
        for (store, m), value in zip(keys, lax.optimization_barrier([s[m] for s, m in keys])):
            store[m] = value

    def compute(masks):
        for at in range(0, len(masks), most):
            some = masks[at : at + most]
            parts.update(zip(some, experts_on([held[m] for m in some])))

    def send_home(masks):
        home.update((m, exchange(parts[m], 2 * m) if m else parts[m]) for m in masks)

    def fetch(masks):
        for m in masks:
            held[m] = exchange(held[m ^ hop_of(m)], 2 * hop_of(m))

    fetch(of[1])
    near = of[1][-1]
    held[near], down = lax.optimization_barrier((held[near], down))
    compute(of[0])
    send_home(of[0])
    crossing = [m for m in of[2] if hop_of(m) >= minor and m & (minor - 1)]
    held[near] = pl.pallas_call(
        gate_body,
        out_shape=jax.ShapeDtypeStruct(packed.shape, packed.dtype),
        in_specs=[anywhere] * 2,
        out_specs=anywhere,
        input_output_aliases={1: 0},
        compiler_params=pltpu.CompilerParams(vmem_limit_bytes=1 << 20),
        cost_estimate=pl.CostEstimate(flops=0, bytes_accessed=0, transcendentals=0),
    )(parts[0], held[near])
    fetch(crossing)
    tie((held, [m for m in of[1] if m >= minor]), (parts, of[0]))
    fetch([m for m in of[2] if m not in crossing])
    first = sorted(of[1], key=lambda m: (m < minor, m))
    compute(first)
    send_home(of[1])
    for stage in range(3, stages):
        fetch(of[stage])
        compute(of[stage - 1])
        send_home(of[stage - 1])
    last = sorted(of[-1], key=lambda m: (m not in crossing, hop_of(m) >= minor, -m))
    compute(last)
    send_home([m for m in last if m >= 2 * minor] + [m for m in last if m < 2 * minor])
    partial = list(home.values())
    return small(sum_body, (rows, hidden_units), chips, 8, 2000000)(*partial)


def solution(mesh):
    placed = (
        P(("groups", "expert"), None),
        P(("groups", "expert"), None),
        P(("groups", "expert"), None),
        P(),
        P("expert", None, None),
        P("expert", None, None),
    )
    return jax.shard_map(
        shards, mesh=mesh, in_specs=placed, out_specs=P(("groups", "expert"), None), check_vma=False
    )
```
